32 devices in a mesh: groups: 2 (over x), band: 16 (over z, y, core).
Axes of the slice: x: 2, y: 2, z: 4, core: 2. Of those that a mesh axis runs over, the one named last changes fastest.
Arguments:
- grid_latent: bfloat16 [24576, 512], P(('groups', 'band')), parts along dimension 0, may hold values from -6 to 6
- mesh_latent: bfloat16 [5120, 512], P(('groups', 'band')), parts along dimension 0, may hold values from -6 to 6
- grid_edges: bfloat16 [24576, 512], P('band'), may hold values from -6 to 6
- mesh_edges: bfloat16 [16384, 512], P('band'), may hold values from -6 to 6
- grid_slots: int32 [16, 16, 96], P('band'), may hold values from -1 to 767, as said below
- grid_senders: int32 [24576], P('band'), may hold values from 0 to 1535, as said below
- grid_receivers: int32 [24576], P('band'), may hold values from 0 to 160, as said below
- mesh_slots: int32 [16, 16, 32], P('band'), may hold values from -1 to 159, as said below
- mesh_senders: int32 [16384], P('band'), may hold values from 0 to 751, as said below
- mesh_receivers: int32 [16384], P('band'), may hold values from 0 to 160, as said below
- grid_node_in: bfloat16 [512, 512], replicated, may hold values from -0.25 to 0.25
- grid_node_out: bfloat16 [512, 512], replicated, may hold values from -0.25 to 0.25
- grid_node_vectors: float32 [2, 512], replicated, may hold values from -4 to 4
- encode_edge_in: bfloat16 [1536, 512], replicated, may hold values from -0.15625 to 0.15625
- encode_edge_out: bfloat16 [512, 512], replicated, may hold values from -0.25 to 0.25
- encode_edge_vectors: float32 [2, 512], replicated, may hold values from -4 to 4
- encode_node_in: bfloat16 [1024, 512], replicated, may hold values from -0.1875 to 0.1875
- encode_node_out: bfloat16 [512, 512], replicated, may hold values from -0.25 to 0.25
- encode_node_vectors: float32 [2, 512], replicated, may hold values from -4 to 4
- process_edge_in: bfloat16 [1536, 512], replicated, may hold values from -0.15625 to 0.15625
- process_edge_out: bfloat16 [512, 512], replicated, may hold values from -0.25 to 0.25
- process_edge_vectors: float32 [2, 512], replicated, may hold values from -4 to 4
- process_node_in: bfloat16 [1024, 512], replicated, may hold values from -0.1875 to 0.1875
- process_node_out: bfloat16 [512, 512], replicated, may hold values from -0.25 to 0.25
- process_node_vectors: float32 [2, 512], replicated, may hold values from -4 to 4
Outputs:
- grid_update: bfloat16 [24576, 512], P(('groups', 'band')), parts along dimension 0
- mesh_update: bfloat16 [5120, 512], P(('groups', 'band')), parts along dimension 0
The draws below stay inside these ranges and needn't reach their ends.
There are 2 independent parts, one for each index of `groups`. The reference program is written for one: setup_inputs(seed, part) draws one part's arguments, and reference() takes and returns one part's arrays. A program takes and returns all parts, laid end to end along the dimension named above; an argument that names none is the same for every part. Nothing has to cross between parts.
Inputs may be any that keep to these rules, and one draw needn't show every extreme that they name: `grid_slots`: entry [s, d, k] is the row among device s's 768 grid rows that device s sends to device d in slot k, or -1 for an empty slot. In every pair the live slots come first and there is at least one; one destination gets all 96 slots from every source, and one source fills all 96 slots to every destination. `grid_senders`: each code is src * 96 + k where k is a live slot that device src sends to the edge's device; every device has edges reading from every source. `grid_receivers`: 160 marks a padding edge. Padding edges stand at the end of each device's 1536 rows, at least half of each device's rows are live, and some device has no padding. `mesh_slots`: entry [s, d, k] is the row among device s's 160 mesh rows that device s sends to device d in slot k, or -1 for an empty slot. In every pair the live slots come first and there is at least one; one destination gets all 32 slots from every source, and one source fills all 32 slots to every destination. `mesh_senders`: A code below 240 names one of the device's own rows or one of the 40 rows at the near end of a neighbouring device; the first device reads no row before its own, the last none after. A larger code is 240 + src * 32 + k with k a live slot that device src sends to the edge's device; every device has edges reading from every source. `mesh_receivers`: 160 marks a padding edge. Padding edges stand at the end of each device's 1024 rows, at least half of each device's rows are live, and some device has no padding.
All inputs are finite; a program needn't handle non-finite values.
Results may differ from the reference program's by a relative error of at most 0.008.
Values may be sent and summed in bfloat16 or wider, within the bound.
A program may use at most 64 MiB of HBM per device.

```python
import jax
import jax.numpy as jnp
from jax import lax

L = 512
G_DEV = 768
M_DEV = 160
EG_DEV = 1536
EM_DEV = 1024
CAP_G = 96
CAP_M = 32
RIM = 40
GRID = 12288
MESH = 2560
EGRID = 24576
EMESH = 16384
N_BAND = 16


def slot_counts(key_list, capacity):
    band_index = jnp.arange(N_BAND, dtype=jnp.int32)
    counts = jax.random.randint(key_list[0], (N_BAND, N_BAND), 1, capacity + 1)
    full_target = jax.random.randint(key_list[1], (), 0, N_BAND)
    full_source = jax.random.randint(key_list[2], (), 0, N_BAND)
    counts = jnp.where(band_index[None, :] == full_target, capacity, counts)
    counts = jnp.where(band_index[:, None] == full_source, capacity, counts)
    return counts


def slot_table(key_list, counts, capacity, row_limit):
    row_pick = jax.random.randint(key_list[3], (N_BAND, N_BAND, capacity), 0, row_limit)
    position = jnp.arange(capacity, dtype=jnp.int32)
    return jnp.where(position[None, None, :] < counts[:, :, None], row_pick, -1)


def far_codes(key_list, counts, capacity, edge_rows):
    band_index = jnp.arange(N_BAND, dtype=jnp.int32)
    edge_index = jnp.arange(edge_rows, dtype=jnp.int32)[None, :]
    offset = jax.random.randint(key_list[4], (N_BAND, 1), 0, N_BAND)
    random_source = jax.random.randint(key_list[5], (N_BAND, edge_rows), 0, N_BAND)
    source = jnp.where(edge_index < N_BAND, (edge_index + offset) % N_BAND, random_source)
    available = counts[source, band_index[:, None]]
    slot_pick = jax.random.randint(key_list[6], (N_BAND, edge_rows), 0, available)
    full_target = jax.random.randint(key_list[1], (), 0, N_BAND)
    forced = (band_index[:, None] == full_target) & (edge_index < N_BAND)
    slot_pick = jnp.where(forced & (source == N_BAND - 1), capacity - 1, slot_pick)
    slot_pick = jnp.where(forced & (source == 0), 0, slot_pick)
    return source * capacity + slot_pick


def receiver_rows(key_list, edge_rows):
    band_index = jnp.arange(N_BAND, dtype=jnp.int32)
    edge_index = jnp.arange(edge_rows, dtype=jnp.int32)[None, :]
    live_count = jax.random.randint(key_list[7], (N_BAND, 1), edge_rows // 2, edge_rows + 1)
    busy_band = jax.random.randint(key_list[8], (), 0, N_BAND)
    live_count = jnp.where(band_index[:, None] == busy_band, edge_rows, live_count)
    chosen = jax.random.randint(key_list[9], (N_BAND, edge_rows), 0, M_DEV)
    return jnp.where(edge_index < live_count, chosen, M_DEV)


def grid_graph(key):
    key = jax.random.fold_in(key, 101)
    key_list = jax.random.split(key, 12)
    counts = slot_counts(key_list, CAP_G)
    table = slot_table(key_list, counts, CAP_G, G_DEV)
    senders = far_codes(key_list, counts, CAP_G, EG_DEV)
    receivers = receiver_rows(key_list, EG_DEV)
    return (table, senders.reshape(-1), receivers.reshape(-1))


def mesh_graph(key):
    key = jax.random.fold_in(key, 202)
    key_list = jax.random.split(key, 12)
    band_index = jnp.arange(N_BAND, dtype=jnp.int32)
    edge_index = jnp.arange(EM_DEV, dtype=jnp.int32)[None, :]
    counts = slot_counts(key_list, CAP_M)
    table = slot_table(key_list, counts, CAP_M, M_DEV)
    near_limit = M_DEV + 2 * RIM
    far_part = near_limit + far_codes(key_list, counts, CAP_M, EM_DEV)
    lowest = jnp.where(band_index == 0, RIM, 0)[:, None]
    highest = jnp.where(band_index == N_BAND - 1, M_DEV + RIM, near_limit)[:, None]
    near_part = jax.random.randint(key_list[10], (N_BAND, EM_DEV), lowest, highest)
    near_part = jnp.where((band_index[:, None] == 1) & (edge_index == N_BAND), 0, near_part)
    far_pick = jax.random.randint(key_list[11], (N_BAND, EM_DEV), 0, 2)
    far_pick = jnp.where((band_index[:, None] == 1) & (edge_index == N_BAND), 1, far_pick)
    senders = jnp.where((edge_index < N_BAND) | (far_pick == 0), far_part, near_part)
    receivers = receiver_rows(key_list, EM_DEV)
    return (table, senders.reshape(-1), receivers.reshape(-1))


def draw_grid_slots(key, part):
    return grid_graph(key)[0]


def draw_grid_senders(key, part):
    return grid_graph(key)[1]


def draw_grid_receivers(key, part):
    return grid_graph(key)[2]


def draw_mesh_slots(key, part):
    return mesh_graph(key)[0]


def draw_mesh_senders(key, part):
    return mesh_graph(key)[1]


def draw_mesh_receivers(key, part):
    return mesh_graph(key)[2]


def shard_levels(rng, dims, shards, least, top_value):
    gain = 1.0
    for axis_at, blocks in shards:
        draws = jax.random.uniform(jax.random.fold_in(jax.random.fold_in(rng, 6), axis_at), (blocks,), jnp.float32, least / len(shards), top_value / len(shards))
        gain = gain * jnp.repeat(jnp.exp(draws), dims[axis_at] // blocks).reshape((-1,) + (1,) * (len(dims) - 1 - axis_at))
    return gain


def scatter_about(own_key, extent, scale, reach, pieces=(), held_as=jnp.bfloat16):
    values = jax.random.normal(own_key, extent, jnp.float32) * scale
    if len(pieces) > 0:
        values = shard_levels(own_key, extent, pieces, -0.22, 0.18) * values
    return jnp.clip(values, min=-reach, max=reach).astype(held_as)


def setup_inputs(seed: int = 0, part: int = 0) -> dict:
    streams_of = jax.random.split(jax.random.key(seed), 26)
    own_keys = jax.random.split(jax.random.fold_in(streams_of[25], part), 26)
    grid_latent = scatter_about(own_keys[0], (GRID, L), 1.0, 6.0, ((0, 16),))
    mesh_latent = scatter_about(own_keys[1], (MESH, L), 1.0, 6.0, ((0, 16),))
    grid_edges = scatter_about(streams_of[2], (EGRID, L), 1.0, 6.0, ((0, 16),))
    mesh_edges = scatter_about(streams_of[3], (EMESH, L), 1.0, 6.0, ((0, 16),))
    grid_slots = draw_grid_slots(jax.random.fold_in(streams_of[25], 71), part)
    grid_senders = draw_grid_senders(jax.random.fold_in(streams_of[25], 71), part)
    grid_receivers = draw_grid_receivers(jax.random.fold_in(streams_of[25], 71), part)
    mesh_slots = draw_mesh_slots(jax.random.fold_in(streams_of[25], 71), part)
    mesh_senders = draw_mesh_senders(jax.random.fold_in(streams_of[25], 71), part)
    mesh_receivers = draw_mesh_receivers(jax.random.fold_in(streams_of[25], 71), part)
    grid_node_in = scatter_about(streams_of[10], (L, L), L ** -0.5, 0.25)
    grid_node_out = scatter_about(streams_of[11], (L, L), L ** -0.5, 0.25)
    grid_node_vectors = scatter_about(streams_of[12], (2, L), 1.0, 4.0, (), jnp.float32)
    encode_edge_in = scatter_about(streams_of[13], (3 * L, L), (3 * L) ** -0.5, 0.15625)
    encode_edge_out = scatter_about(streams_of[14], (L, L), L ** -0.5, 0.25)
    encode_edge_vectors = scatter_about(streams_of[15], (2, L), 1.0, 4.0, (), jnp.float32)
    encode_node_in = scatter_about(streams_of[16], (2 * L, L), (2 * L) ** -0.5, 0.1875)
    encode_node_out = scatter_about(streams_of[17], (L, L), L ** -0.5, 0.25)
    encode_node_vectors = scatter_about(streams_of[18], (2, L), 1.0, 4.0, (), jnp.float32)
    process_edge_in = scatter_about(streams_of[19], (3 * L, L), (3 * L) ** -0.5, 0.15625)
    process_edge_out = scatter_about(streams_of[20], (L, L), L ** -0.5, 0.25)
    process_edge_vectors = scatter_about(streams_of[21], (2, L), 1.0, 4.0, (), jnp.float32)
    process_node_in = scatter_about(streams_of[22], (2 * L, L), (2 * L) ** -0.5, 0.1875)
    process_node_out = scatter_about(streams_of[23], (L, L), L ** -0.5, 0.25)
    process_node_vectors = scatter_about(streams_of[24], (2, L), 1.0, 4.0, (), jnp.float32)
    return {"grid_latent": grid_latent, "mesh_latent": mesh_latent, "grid_edges": grid_edges, "mesh_edges": mesh_edges, "grid_slots": grid_slots, "grid_senders": grid_senders, "grid_receivers": grid_receivers, "mesh_slots": mesh_slots, "mesh_senders": mesh_senders, "mesh_receivers": mesh_receivers, "grid_node_in": grid_node_in, "grid_node_out": grid_node_out, "grid_node_vectors": grid_node_vectors, "encode_edge_in": encode_edge_in, "encode_edge_out": encode_edge_out, "encode_edge_vectors": encode_edge_vectors, "encode_node_in": encode_node_in, "encode_node_out": encode_node_out, "encode_node_vectors": encode_node_vectors, "process_edge_in": process_edge_in, "process_edge_out": process_edge_out, "process_edge_vectors": process_edge_vectors, "process_node_in": process_node_in, "process_node_out": process_node_out, "process_node_vectors": process_node_vectors}


def mlp_tail(preact, vectors, weight_out):
    hidden = jax.nn.silu(preact + vectors[0]).astype(jnp.bfloat16)
    output = jnp.dot(hidden, weight_out, preferred_element_type=jnp.float32)
    centred = output - lax.optimization_barrier(jnp.mean(output, axis=-1, keepdims=True))
    spread = lax.optimization_barrier(jnp.mean(centred * centred, axis=-1, keepdims=True))
    return centred * lax.rsqrt(spread + 1e-05) * vectors[1]

def edge_sums(sender_terms, edge_latent, receivers, receiver_terms, edge_weight, vectors, weight_out):
    preact = jnp.dot(edge_latent, edge_weight, preferred_element_type=jnp.float32)
    preact = preact + sender_terms.astype(jnp.float32)
    preact = preact + receiver_terms[jnp.minimum(receivers, M_DEV - 1)]
    message = (edge_latent.astype(jnp.float32) + mlp_tail(preact, vectors, weight_out)).astype(jnp.bfloat16)
    totals = jax.ops.segment_sum(message.astype(jnp.float32), receivers, num_segments=M_DEV + 1)
    return totals[:M_DEV]

def reference(grid_latent, mesh_latent, grid_edges, mesh_edges, grid_slots, grid_senders, grid_receivers, mesh_slots, mesh_senders, mesh_receivers, grid_node_in, grid_node_out, grid_node_vectors, encode_edge_in, encode_edge_out, encode_edge_vectors, encode_node_in, encode_node_out, encode_node_vectors, process_edge_in, process_edge_out, process_edge_vectors, process_node_in, process_node_out, process_node_vectors):
    latent_width = grid_latent.shape[1]
    band_index = jnp.arange(N_BAND, dtype=jnp.int32)[:, None]
    grid_preact = jnp.dot(grid_latent, grid_node_in, preferred_element_type=jnp.float32)
    grid_update = (grid_latent.astype(jnp.float32) + mlp_tail(grid_preact, grid_node_vectors, grid_node_out)).astype(jnp.bfloat16)
    grid_terms = jnp.dot(grid_latent, encode_edge_in[latent_width:2 * latent_width], preferred_element_type=jnp.float32).astype(jnp.bfloat16)
    sender_codes = grid_senders.reshape(N_BAND, EG_DEV)
    source = sender_codes // CAP_G
    sender_rows = source * G_DEV + grid_slots[source, band_index, sender_codes % CAP_G]
    receiver_terms = jnp.dot(mesh_latent, encode_edge_in[2 * latent_width:], preferred_element_type=jnp.float32)
    receiver_terms = receiver_terms.reshape(N_BAND, M_DEV, latent_width)

    def encode(inputs):
        rows_here, latent_here, receivers_here, terms_here = inputs
        return edge_sums(grid_terms[rows_here], latent_here, receivers_here, terms_here, encode_edge_in[:latent_width], encode_edge_vectors, encode_edge_out)
    encode_sum = lax.map(encode, (sender_rows, grid_edges.reshape(N_BAND, EG_DEV, latent_width), grid_receivers.reshape(N_BAND, EG_DEV), receiver_terms))
    encode_rounded = encode_sum.reshape(N_BAND * M_DEV, latent_width).astype(jnp.bfloat16)
    node_preact = jnp.dot(mesh_latent, encode_node_in[:latent_width], preferred_element_type=jnp.float32)
    node_preact = node_preact + jnp.dot(encode_rounded, encode_node_in[latent_width:], preferred_element_type=jnp.float32)
    mesh_middle = (mesh_latent.astype(jnp.float32) + mlp_tail(node_preact, encode_node_vectors, encode_node_out)).astype(jnp.bfloat16)
    mesh_terms = jnp.dot(mesh_middle, process_edge_in[latent_width:2 * latent_width], preferred_element_type=jnp.float32).astype(jnp.bfloat16)
    sender_codes = mesh_senders.reshape(N_BAND, EM_DEV)
    near_limit = M_DEV + 2 * RIM
    far_code = jnp.maximum(sender_codes - near_limit, 0)
    source = far_code // CAP_M
    far_rows = source * M_DEV + mesh_slots[source, band_index, far_code % CAP_M]
    near_rows = band_index * M_DEV - RIM + sender_codes
    mesh_rows = jnp.where(sender_codes < near_limit, near_rows, far_rows)
    middle_terms = jnp.dot(mesh_middle, process_edge_in[2 * latent_width:], preferred_element_type=jnp.float32)
    middle_terms = middle_terms.reshape(N_BAND, M_DEV, latent_width)

    def process(inputs):
        rows_here, latent_here, receivers_here, terms_here = inputs
        return edge_sums(mesh_terms[rows_here], latent_here, receivers_here, terms_here, process_edge_in[:latent_width], process_edge_vectors, process_edge_out)
    process_sum = lax.map(process, (mesh_rows, mesh_edges.reshape(N_BAND, EM_DEV, latent_width), mesh_receivers.reshape(N_BAND, EM_DEV), middle_terms))
    process_rounded = process_sum.reshape(N_BAND * M_DEV, latent_width).astype(jnp.bfloat16)
    final_preact = jnp.dot(mesh_middle, process_node_in[:latent_width], preferred_element_type=jnp.float32)
    final_preact = final_preact + jnp.dot(process_rounded, process_node_in[latent_width:], preferred_element_type=jnp.float32)
    mesh_update = (mesh_middle.astype(jnp.float32) + mlp_tail(final_preact, process_node_vectors, process_node_out)).astype(jnp.bfloat16)
    return (grid_update, mesh_update)
```

```python
import functools
import typing
from typing import Any

import jax
import jax.numpy as jnp
from jax import lax
from jax.experimental import pallas as pl
from jax.experimental.pallas import tpu as pltpu
from jax.sharding import PartitionSpec as P

MESH = pl.DeviceIdType.MESH
BF = jnp.bfloat16
F32 = jnp.float32
BLOCK = 256

class Operands(typing.NamedTuple):
    grid_latent: Any
    mesh_latent: Any
    grid_edges: Any
    mesh_edges: Any
    grid_slots: Any
    grid_senders: Any
    grid_receivers: Any
    mesh_slots: Any
    mesh_senders: Any
    mesh_receivers: Any
    grid_node_in: Any
    grid_node_out: Any
    grid_node_vectors: Any
    encode_edge_in: Any
    encode_edge_out: Any
    encode_edge_vectors: Any
    encode_node_in: Any
    encode_node_out: Any
    encode_node_vectors: Any
    process_edge_in: Any
    process_edge_out: Any
    process_edge_vectors: Any
    process_node_in: Any
    process_node_out: Any
    process_node_vectors: Any


COUNT = len(Operands._fields)


def round_up(value, unit):
    return (value + unit - 1) // unit * unit


def group_size(count, rows):
    size = 1
    while size * 2 <= count and size * 2 * rows <= BLOCK:
        size *= 2
    return size


def dot(left, right):
    return jnp.dot(left, right, preferred_element_type=F32)


def branch(preact, vectors, weight_out):
    half = 0.5 * (preact + vectors[0:1, :])
    hidden = (half + half * jnp.tanh(half)).astype(BF)
    output = dot(hidden, weight_out[...])
    centred = output - jnp.mean(output, axis=-1, keepdims=True)
    spread = jnp.mean(centred * centred, axis=-1, keepdims=True)
    return centred * lax.rsqrt(spread + 1e-05) * vectors[1:2, :]


def column(row):
    n = row.shape[1]
    eye = lax.broadcasted_iota(jnp.int32, (n, n), 0) == lax.broadcasted_iota(
        jnp.int32, (n, n), 1
    )
    spread = jnp.where(eye, jnp.broadcast_to(row.astype(F32), (n, n)), 0.0)
    return jnp.sum(spread, axis=1, keepdims=True)


def onehot_rows(col, width):
    ids = lax.broadcasted_iota(jnp.int32, (1, width), 1).astype(F32)
    return jnp.where(col == ids, 1.0, 0.0).astype(BF)


def onehot_columns(row, height):
    ids = lax.broadcasted_iota(jnp.int32, (height, 1), 0).astype(F32)
    return jnp.where(ids == row.astype(F32), 1.0, 0.0).astype(BF)


def rows_at(start, size, unit=16):
    return pl.ds(pl.multiple_of(start, unit), size)


def kernel(dims, *refs):
    count, cap_g, cap_m = dims
    n_in = COUNT
    hbm = Operands(*refs[:n_in])
    grid_out, mesh_out = refs[n_in : n_in + 2]
    held = Operands(*refs[n_in + 2 : 2 * n_in + 2])
    (
        own_terms,
        send_g,
        arrived,
        sender_hot,
        receiver_hot,
        sum_hot,
        preact,
        message,
        grid_result,
        send_m,
        table,
        sender_hot_m,
        receiver_hot_m,
        sum_hot_m,
        pick_hot_m,
        preact_m,
        mesh_result,
        fetch_sem,
        out_sem,
        send_sem,
        recv_sem,
        send_sem_m,
        recv_sem_m,
        send_sem_rim,
        recv_sem_rim,
    ) = refs[2 * n_in + 2 :]
    me = lax.axis_index("band")
    width = held.grid_latent.shape[1]
    grid_rows = held.grid_latent.shape[0]
    mesh_rows = held.mesh_latent.shape[0]
    grid_edge_rows = held.grid_edges.shape[0]
    mesh_edge_rows = held.mesh_edges.shape[0]
    rim = mesh_rows // 4
    rim_held = round_up(rim, 16)
    near = mesh_rows + 2 * rim_held

    copies = Operands(
        *[
            pltpu.make_async_copy(hbm[index], held[index], fetch_sem.at[index])
            for index in range(n_in)
        ]
    )
    for copy in (
        copies.grid_slots,
        copies.grid_latent,
        copies.encode_edge_in,
        copies.grid_senders,
        copies.grid_receivers,
        copies.mesh_latent,
        copies.grid_edges,
        copies.grid_node_in,
        copies.grid_node_vectors,
        copies.grid_node_out,
        copies.mesh_slots,
        copies.mesh_senders,
        copies.mesh_receivers,
        copies.mesh_edges,
        copies.process_edge_in,
        copies.encode_node_in,
        copies.encode_edge_vectors,
        copies.encode_edge_out,
        copies.encode_node_vectors,
        copies.encode_node_out,
        copies.process_edge_vectors,
        copies.process_edge_out,
        copies.process_node_in,
        copies.process_node_vectors,
        copies.process_node_out,
    ):
        copy.start()

    barrier = pltpu.get_barrier_semaphore()

    @pl.loop(1, count)
    def _(step):
        pl.semaphore_signal(
            barrier,
            inc=1,
            device_id={"band": lax.rem(me + step, count)},
            device_id_type=MESH,
        )

    def ready(*wanted):
        for copy in wanted:
            copy.wait()

    ready(copies.grid_slots, copies.grid_latent, copies.encode_edge_in)

    @pl.loop(0, grid_rows // BLOCK)
    def _(step):
        rows = rows_at(step * BLOCK, BLOCK)
        own_terms[rows, :] = dot(
            held.grid_latent[rows, :], held.encode_edge_in[width : 2 * width, :]
        ).astype(BF)

    pl.semaphore_wait(barrier, count - 1)

    size_g = group_size(count, cap_g)
    groups_g = count // size_g
    my_group = me // size_g
    own_slot = (groups_g - 1) * size_g + lax.rem(me, size_g)

    def grid_copy(target, slot):
        return pltpu.make_async_remote_copy(
            src_ref=send_g.at[rows_at(target * cap_g, cap_g)],
            dst_ref=arrived.at[rows_at(slot * cap_g, cap_g)],
            send_sem=send_sem.at[target],
            recv_sem=recv_sem.at[slot],
            device_id={"band": target},
            device_id_type=MESH,
        )

    @pl.loop(0, groups_g)
    def _(step):
        group = lax.rem(my_group + groups_g // 2 + step, groups_g)
        hot = [
            onehot_rows(
                column(held.grid_slots[pl.ds(group * size_g + j, 1), :]), grid_rows
            )
            for j in range(size_g)
        ]
        hot = jnp.concatenate(hot, axis=0) if size_g > 1 else hot[0]
        picked = dot(hot, own_terms[...]).astype(BF)
        send_g[rows_at(group * size_g * cap_g, size_g * cap_g), :] = picked
        slot = (
            lax.rem(my_group - group - 1 + 2 * groups_g, groups_g) * size_g
            + lax.rem(me, size_g)
        )

        @pl.loop(0, size_g)
        def _(j):
            target = group * size_g + j

            @pl.when(target != me)
            def _():
                grid_copy(target, slot).start()

    arrived[rows_at(own_slot * cap_g, cap_g), :] = send_g[rows_at(me * cap_g, cap_g), :]

    ready(copies.grid_senders, copies.grid_receivers, copies.mesh_latent, copies.grid_edges)
    receiver_terms = dot(
        held.mesh_latent[...], held.encode_edge_in[2 * width :, :]
    ).astype(BF)
    base = (my_group + 1) * size_g * cap_g

    @pl.loop(0, grid_edge_rows // 128)
    def _(step):
        rows = rows_at(step * 128, 128, 128)
        codes = held.grid_senders[pl.ds(step, 1), :] - base
        codes = jnp.where(codes < 0, codes + count * cap_g, codes)
        sender_hot[rows, :] = onehot_rows(column(codes), count * cap_g)
        receivers = held.grid_receivers[pl.ds(step, 1), :]
        receiver_hot[rows, :] = onehot_rows(column(receivers), mesh_rows)
        sum_hot[:, rows] = onehot_columns(receivers, mesh_rows)

    @pl.loop(0, grid_edge_rows // BLOCK)
    def _(step):
        rows = rows_at(step * BLOCK, BLOCK)
        preact[rows, :] = dot(
            held.grid_edges[rows, :], held.encode_edge_in[:width, :]
        ) + dot(receiver_hot[rows, :], receiver_terms)

    ready(copies.grid_node_in, copies.grid_node_vectors, copies.grid_node_out)

    @pl.loop(0, grid_rows // BLOCK)
    def _(step):
        rows = rows_at(step * BLOCK, BLOCK)
        latent = held.grid_latent[rows, :]
        update = branch(
            dot(latent, held.grid_node_in[...]),
            held.grid_node_vectors,
            held.grid_node_out,
        )
        grid_result[rows, :] = (latent.astype(F32) + update).astype(BF)

    grid_store = pltpu.make_async_copy(grid_result, grid_out, out_sem.at[0])
    grid_store.start()

    ready(copies.mesh_slots, copies.mesh_senders, copies.mesh_receivers, copies.mesh_edges, copies.process_edge_in)
    near_codes = mesh_rows + 2 * rim

    @pl.loop(0, mesh_edge_rows // 128)
    def _(step):
        rows = rows_at(step * 128, 128, 128)
        codes = held.mesh_senders[pl.ds(step, 1), :]
        shift = rim_held - rim
        codes = codes + jnp.where(codes < near_codes, shift, 2 * shift)
        sender_hot_m[rows, :] = onehot_rows(column(codes), near + count * cap_m)
        receivers = held.mesh_receivers[pl.ds(step, 1), :]
        receiver_hot_m[rows, :] = onehot_rows(column(receivers), mesh_rows)
        sum_hot_m[:, rows] = onehot_columns(receivers, mesh_rows)

    @pl.loop(0, count)
    def _(step):
        slots = held.mesh_slots[pl.ds(step, 1), :]
        pick_hot_m[rows_at(step * cap_m, cap_m), :] = onehot_rows(column(slots), mesh_rows)

    @pl.loop(0, mesh_edge_rows // BLOCK)
    def _(step):
        rows = rows_at(step * BLOCK, BLOCK)
        preact_m[rows, :] = dot(
            held.mesh_edges[rows, :], held.process_edge_in[:width, :]
        )

    ready(copies.encode_node_in)
    node_preact = dot(held.mesh_latent[...], held.encode_node_in[:width, :])
    ready(copies.encode_edge_vectors, copies.encode_edge_out, copies.encode_node_vectors, copies.encode_node_out)

    part = count // 2

    def wait_for(first, last):
        @pl.loop(first, last)
        def _(slot):
            @pl.when(slot != own_slot)
            def _():
                grid_copy(lax.rem(me + 1, count), slot).wait_recv()

    wait_for(0, part)

    @pl.loop(0, grid_edge_rows // BLOCK)
    def _(step):
        rows = rows_at(step * BLOCK, BLOCK)
        preact[rows, :] += dot(sender_hot[rows, : part * cap_g], arrived[: part * cap_g, :])

    wait_for(part, count)

    @pl.loop(0, grid_edge_rows // BLOCK)
    def _(step):
        rows = rows_at(step * BLOCK, BLOCK)
        total = preact[rows, :] + dot(
            sender_hot[rows, part * cap_g :], arrived[part * cap_g :, :]
        )
        update = branch(total, held.encode_edge_vectors, held.encode_edge_out)
        message[rows, :] = (held.grid_edges[rows, :].astype(F32) + update).astype(BF)

    encode_sum = dot(sum_hot[...], message[...]).astype(BF)
    node_preact = node_preact + dot(encode_sum, held.encode_node_in[width:, :])
    middle = (
        held.mesh_latent[...].astype(F32)
        + branch(node_preact, held.encode_node_vectors, held.encode_node_out)
    ).astype(BF)

    own_mesh = dot(middle, held.process_edge_in[width : 2 * width, :]).astype(BF)
    table[rim_held : rim_held + mesh_rows, :] = own_mesh

    def far_copy(target, source):
        return pltpu.make_async_remote_copy(
            src_ref=send_m.at[rows_at(target * cap_m, cap_m)],
            dst_ref=table.at[rows_at(near + source * cap_m, cap_m)],
            send_sem=send_sem_m.at[target],
            recv_sem=recv_sem_m.at[source],
            device_id={"band": target},
            device_id_type=MESH,
        )

    size_m = group_size(count, cap_m)
    groups_m = count // size_m

    @pl.loop(0, groups_m)
    def _(step):
        group = lax.rem(me // size_m + 1 + step, groups_m)
        rows = rows_at(group * size_m * cap_m, size_m * cap_m)
        send_m[rows, :] = dot(pick_hot_m[rows, :], own_mesh).astype(BF)

        @pl.loop(0, size_m)
        def _(j):
            target = group * size_m + j

            @pl.when(target != me)
            def _():
                far_copy(target, me).start()

    to_right = pltpu.make_async_remote_copy(
        src_ref=table.at[pl.ds(rim_held + mesh_rows - rim_held, rim_held)],
        dst_ref=table.at[pl.ds(0, rim_held)],
        send_sem=send_sem_rim.at[0],
        recv_sem=recv_sem_rim.at[0],
        device_id={"band": lax.rem(me + 1, count)},
        device_id_type=MESH,
    )
    to_left = pltpu.make_async_remote_copy(
        src_ref=table.at[pl.ds(rim_held, rim_held)],
        dst_ref=table.at[pl.ds(rim_held + mesh_rows, rim_held)],
        send_sem=send_sem_rim.at[1],
        recv_sem=recv_sem_rim.at[1],
        device_id={"band": lax.rem(me + count - 1, count)},
        device_id_type=MESH,
    )
    to_right.start()
    to_left.start()
    table[rows_at(near + me * cap_m, cap_m), :] = send_m[rows_at(me * cap_m, cap_m), :]

    middle_terms = dot(middle, held.process_edge_in[2 * width :, :]).astype(BF)

    @pl.loop(0, mesh_edge_rows // BLOCK)
    def _(step):
        rows = rows_at(step * BLOCK, BLOCK)
        preact_m[rows, :] += dot(receiver_hot_m[rows, :], middle_terms)

    ready(copies.process_edge_vectors, copies.process_edge_out)
    ready(copies.process_node_in, copies.process_node_vectors, copies.process_node_out)
    node_preact = dot(middle, held.process_node_in[:width, :])

    to_right.wait_recv()
    to_left.wait_recv()

    @pl.loop(0, count)
    def _(source):
        @pl.when(source != me)
        def _():
            far_copy(lax.rem(me + 1, count), source).wait_recv()

    @pl.loop(0, mesh_edge_rows // BLOCK)
    def _(step):
        rows = rows_at(step * BLOCK, BLOCK)
        total = preact_m[rows, :] + dot(sender_hot_m[rows, :], table[...])
        update = branch(total, held.process_edge_vectors, held.process_edge_out)
        message[rows, :] = (held.mesh_edges[rows, :].astype(F32) + update).astype(BF)

    process_sum = dot(sum_hot_m[...], message[:mesh_edge_rows, :]).astype(BF)
    node_preact = node_preact + dot(process_sum, held.process_node_in[width:, :])
    mesh_result[...] = (
        middle.astype(F32)
        + branch(node_preact, held.process_node_vectors, held.process_node_out)
    ).astype(BF)
    mesh_store = pltpu.make_async_copy(mesh_result, mesh_out, out_sem.at[1])
    mesh_store.start()

    @pl.loop(0, count)
    def _(target):
        @pl.when(target != me)
        def _():
            grid_copy(target, 0).wait_send()
            far_copy(target, 0).wait_send()

    to_right.wait_send()
    to_left.wait_send()
    grid_store.wait()
    mesh_store.wait()


def pad_slots(slots, cap):
    slots = slots[0]
    if cap == slots.shape[1]:
        return slots
    return jnp.pad(slots, ((0, 0), (0, cap - slots.shape[1])), constant_values=-1)


def spread_codes(codes, slots, cap):
    return codes if cap == slots else codes // slots * cap + codes % slots


def local(*operands):
    args = Operands(*operands)
    count = lax.axis_size("band")
    slots_g = args.grid_slots.shape[2]
    slots_m = args.mesh_slots.shape[2]
    cap_g, cap_m = round_up(slots_g, 16), round_up(slots_m, 16)
    mesh_rows, width = args.mesh_latent.shape
    mesh_senders = args.mesh_senders
    if cap_m != slots_m:
        first = mesh_rows + 2 * (mesh_rows // 4)
        far = first + spread_codes(mesh_senders - first, slots_m, cap_m)
        mesh_senders = jnp.where(mesh_senders < first, mesh_senders, far)
    args = args._replace(
        grid_slots=pad_slots(args.grid_slots, cap_g),
        mesh_slots=pad_slots(args.mesh_slots, cap_m),
        grid_senders=spread_codes(args.grid_senders, slots_g, cap_g).reshape(-1, 128),
        grid_receivers=args.grid_receivers.reshape(-1, 128),
        mesh_senders=mesh_senders.reshape(-1, 128),
        mesh_receivers=args.mesh_receivers.reshape(-1, 128),
    )
    grid_rows = args.grid_latent.shape[0]
    grid_edge_rows = args.grid_edges.shape[0]
    mesh_edge_rows = args.mesh_edges.shape[0]
    near = mesh_rows + 2 * round_up(mesh_rows // 4, 16)
    edge_rows = max(grid_edge_rows, mesh_edge_rows)
    dma = pltpu.SemaphoreType.DMA
    anywhere = pl.BlockSpec(memory_space=pl.ANY)
    scratch = [pltpu.VMEM(arg.shape, arg.dtype) for arg in args]
    scratch += [
        pltpu.VMEM((grid_rows, width), BF),
        pltpu.VMEM((count * cap_g, width), BF),
        pltpu.VMEM((count * cap_g, width), BF),
        pltpu.VMEM((grid_edge_rows, count * cap_g), BF),
        pltpu.VMEM((grid_edge_rows, mesh_rows), BF),
        pltpu.VMEM((mesh_rows, grid_edge_rows), BF),
        pltpu.VMEM((grid_edge_rows, width), F32),
        pltpu.VMEM((edge_rows, width), BF),
        pltpu.VMEM((grid_rows, width), BF),
        pltpu.VMEM((count * cap_m, width), BF),
        pltpu.VMEM((near + count * cap_m, width), BF),
        pltpu.VMEM((mesh_edge_rows, near + count * cap_m), BF),
        pltpu.VMEM((mesh_edge_rows, mesh_rows), BF),
        pltpu.VMEM((mesh_rows, mesh_edge_rows), BF),
        pltpu.VMEM((count * cap_m, mesh_rows), BF),
        pltpu.VMEM((mesh_edge_rows, width), F32),
        pltpu.VMEM((mesh_rows, width), BF),
        dma((COUNT,)),
        dma((2,)),
        dma((count,)),
        dma((count,)),
        dma((count,)),
        dma((count,)),
        dma((2,)),
        dma((2,)),
    ]
    return pl.pallas_call(
        functools.partial(kernel, (count, cap_g, cap_m)),
        out_shape=(
            jax.ShapeDtypeStruct((grid_rows, width), BF),
            jax.ShapeDtypeStruct((mesh_rows, width), BF),
        ),
        in_specs=[anywhere] * COUNT,
        out_specs=(anywhere, anywhere),
        scratch_shapes=scratch,
        compiler_params=pltpu.CompilerParams(
            collective_id=0, has_side_effects=True, vmem_limit_bytes=56 * 1024 * 1024
        ),
    )(*args)


def solution(mesh):
    return jax.shard_map(
        local,
        mesh=mesh,
        in_specs=(
            P(("groups", "band"), None),
            P(("groups", "band"), None),
            P("band", None),
            P("band", None),
            P("band", None, None),
            P("band"),
            P("band"),
            P("band", None, None),
            P("band"),
            P("band"),
            P(),
            P(),
            P(),
            P(),
            P(),
            P(),
            P(),
            P(),
            P(),
            P(),
            P(),
            P(),
            P(),
            P(),
            P(),
        ),
        out_specs=(P(("groups", "band"), None), P(("groups", "band"), None)),
        check_vma=False,
    )
```

```python
import functools
import typing
from typing import Any

import jax
import jax.numpy as jnp
from jax import lax
from jax.experimental import pallas as pl
from jax.experimental.pallas import tpu as pltpu
from jax.sharding import PartitionSpec as P

MESH = pl.DeviceIdType.MESH
BF = jnp.bfloat16
F32 = jnp.float32
BLOCK = 256

class Operands(typing.NamedTuple):
    grid_latent: Any
    mesh_latent: Any
    grid_edges: Any
    mesh_edges: Any
    grid_slots: Any
    grid_senders: Any
    grid_receivers: Any
    mesh_slots: Any
    mesh_senders: Any
    mesh_receivers: Any
    grid_node_in: Any
    grid_node_out: Any
    grid_node_vectors: Any
    encode_edge_in: Any
    encode_edge_out: Any
    encode_edge_vectors: Any
    encode_node_in: Any
    encode_node_out: Any
    encode_node_vectors: Any
    process_edge_in: Any
    process_edge_out: Any
    process_edge_vectors: Any
    process_node_in: Any
    process_node_out: Any
    process_node_vectors: Any


COUNT = len(Operands._fields)


def round_up(value, unit):
    return (value + unit - 1) // unit * unit


def group_size(count, rows):
    size = 1
    while size * 2 <= count and size * 2 * rows <= BLOCK:
        size *= 2
    return size


def dot(left, right):
    return jnp.dot(left, right, preferred_element_type=F32)


def branch(preact, vectors, weight_out):
    half = 0.5 * (preact + vectors[0:1, :])
    hidden = (half + half * jnp.tanh(half)).astype(BF)
    output = dot(hidden, weight_out[...])
    centred = output - jnp.mean(output, axis=-1, keepdims=True)
    spread = jnp.mean(centred * centred, axis=-1, keepdims=True)
    return centred * lax.rsqrt(spread + 1e-05) * vectors[1:2, :]


def column(row):
    n = row.shape[1]
    eye = lax.broadcasted_iota(jnp.int32, (n, n), 0) == lax.broadcasted_iota(
        jnp.int32, (n, n), 1
    )
    spread = jnp.where(eye, jnp.broadcast_to(row.astype(F32), (n, n)), 0.0)
    return jnp.sum(spread, axis=1, keepdims=True)


def onehot_rows(col, width):
    ids = lax.broadcasted_iota(jnp.int32, (1, width), 1).astype(F32)
    return jnp.where(col == ids, 1.0, 0.0).astype(BF)


def onehot_columns(row, height):
    ids = lax.broadcasted_iota(jnp.int32, (height, 1), 0).astype(F32)
    return jnp.where(ids == row.astype(F32), 1.0, 0.0).astype(BF)


def rows_at(start, size, unit=16):
    return pl.ds(pl.multiple_of(start, unit), size)


def kernel(dims, *refs):
    count, cap_g, cap_m = dims
    n_in = COUNT
    hbm = Operands(*refs[:n_in])
    grid_out, mesh_out = refs[n_in : n_in + 2]
    held = Operands(*refs[n_in + 2 : 2 * n_in + 2])
    (
        own_terms,
        send_g,
        arrived,
        sender_hot,
        receiver_hot,
        sum_hot,
        preact,
        message,
        grid_result,
        send_m,
        table,
        sender_hot_m,
        receiver_hot_m,
        sum_hot_m,
        pick_hot_m,
        preact_m,
        mesh_result,
        fetch_sem,
        out_sem,
        send_sem,
        recv_sem,
        send_sem_m,
        recv_sem_m,
        send_sem_rim,
        recv_sem_rim,
    ) = refs[2 * n_in + 2 :]
    me = lax.axis_index("band")
    width = held.grid_latent.shape[1]
    grid_rows = held.grid_latent.shape[0]
    mesh_rows = held.mesh_latent.shape[0]
    grid_edge_rows = held.grid_edges.shape[0]
    mesh_edge_rows = held.mesh_edges.shape[0]
    rim = mesh_rows // 4
    rim_held = round_up(rim, 16)
    near = mesh_rows + 2 * rim_held

    copies = Operands(
        *[
            pltpu.make_async_copy(hbm[index], held[index], fetch_sem.at[index])
            for index in range(n_in)
        ]
    )
    for copy in (
        copies.grid_slots,
        copies.grid_latent,
        copies.encode_edge_in,
        copies.grid_senders,
        copies.grid_receivers,
        copies.mesh_latent,
        copies.grid_edges,
        copies.grid_node_in,
        copies.grid_node_vectors,
        copies.grid_node_out,
        copies.mesh_slots,
        copies.mesh_senders,
        copies.mesh_receivers,
        copies.mesh_edges,
        copies.process_edge_in,
        copies.encode_node_in,
        copies.encode_edge_vectors,
        copies.encode_edge_out,
        copies.encode_node_vectors,
        copies.encode_node_out,
        copies.process_edge_vectors,
        copies.process_edge_out,
        copies.process_node_in,
        copies.process_node_vectors,
        copies.process_node_out,
    ):
        copy.start()

    barrier = pltpu.get_barrier_semaphore()

    @pl.loop(1, count)
    def _(step):
        pl.semaphore_signal(
            barrier,
            inc=1,
            device_id={"band": lax.rem(me + step, count)},
            device_id_type=MESH,
        )

    def ready(*wanted):
        for copy in wanted:
            copy.wait()

    ready(copies.grid_slots, copies.grid_latent, copies.encode_edge_in)

    @pl.loop(0, grid_rows // BLOCK)
    def _(step):
        rows = rows_at(step * BLOCK, BLOCK)
        own_terms[rows, :] = dot(
            held.grid_latent[rows, :], held.encode_edge_in[width : 2 * width, :]
        ).astype(BF)

    pl.semaphore_wait(barrier, count - 1)

    size_g = group_size(count, cap_g)
    groups_g = count // size_g
    my_group = me // size_g
    half_groups = groups_g // 2
    quarter_groups = half_groups // 2
    my_half, my_local = my_group // half_groups, lax.rem(my_group, half_groups)
    my_quarter = my_local // quarter_groups

    def grid_copy(target, source):
        return pltpu.make_async_remote_copy(
            src_ref=send_g.at[rows_at(target * cap_g, cap_g)],
            dst_ref=arrived.at[rows_at(source * cap_g, cap_g)],
            send_sem=send_sem.at[target],
            recv_sem=recv_sem.at[source],
            device_id={"band": target},
            device_id_type=MESH,
        )

    @pl.loop(0, groups_g)
    def _(step):
        half = lax.rem(my_half + 1 + step // half_groups, 2)
        turn = lax.rem(step, half_groups)
        quarter = lax.rem(my_quarter + turn // quarter_groups, 2)
        group = (
            half * half_groups
            + quarter * quarter_groups
            + lax.rem(my_local + turn, quarter_groups)
        )
        hot = [
            onehot_rows(
                column(held.grid_slots[pl.ds(group * size_g + j, 1), :]), grid_rows
            )
            for j in range(size_g)
        ]
        hot = jnp.concatenate(hot, axis=0) if size_g > 1 else hot[0]
        picked = dot(hot, own_terms[...]).astype(BF)
        send_g[rows_at(group * size_g * cap_g, size_g * cap_g), :] = picked
        @pl.loop(0, size_g)
        def _(j):
            target = group * size_g + j

            @pl.when(target != me)
            def _():
                grid_copy(target, me).start()

    arrived[rows_at(me * cap_g, cap_g), :] = send_g[rows_at(me * cap_g, cap_g), :]

    ready(copies.grid_senders, copies.grid_receivers, copies.mesh_latent, copies.grid_edges)
    receiver_terms = dot(
        held.mesh_latent[...], held.encode_edge_in[2 * width :, :]
    ).astype(BF)

    @pl.loop(0, grid_edge_rows // 128)
    def _(step):
        rows = rows_at(step * 128, 128, 128)
        codes = held.grid_senders[pl.ds(step, 1), :]
        sender_hot[rows, :] = onehot_rows(column(codes), count * cap_g)
        receivers = held.grid_receivers[pl.ds(step, 1), :]
        receiver_hot[rows, :] = onehot_rows(column(receivers), mesh_rows)
        sum_hot[:, rows] = onehot_columns(receivers, mesh_rows)

    @pl.loop(0, grid_edge_rows // BLOCK)
    def _(step):
        rows = rows_at(step * BLOCK, BLOCK)
        preact[rows, :] = dot(
            held.grid_edges[rows, :], held.encode_edge_in[:width, :]
        ) + dot(receiver_hot[rows, :], receiver_terms)

    ready(copies.grid_node_in, copies.grid_node_vectors, copies.grid_node_out)

    @pl.loop(0, grid_rows // BLOCK)
    def _(step):
        rows = rows_at(step * BLOCK, BLOCK)
        latent = held.grid_latent[rows, :]
        update = branch(
            dot(latent, held.grid_node_in[...]),
            held.grid_node_vectors,
            held.grid_node_out,
        )
        grid_result[rows, :] = (latent.astype(F32) + update).astype(BF)

    grid_store = pltpu.make_async_copy(grid_result, grid_out, out_sem.at[0])
    grid_store.start()

    ready(copies.mesh_slots, copies.mesh_senders, copies.mesh_receivers, copies.mesh_edges, copies.process_edge_in)
    near_codes = mesh_rows + 2 * rim

    @pl.loop(0, mesh_edge_rows // 128)
    def _(step):
        rows = rows_at(step * 128, 128, 128)
        codes = held.mesh_senders[pl.ds(step, 1), :]
        shift = rim_held - rim
        codes = codes + jnp.where(codes < near_codes, shift, 2 * shift)
        sender_hot_m[rows, :] = onehot_rows(column(codes), near + count * cap_m)
        receivers = held.mesh_receivers[pl.ds(step, 1), :]
        receiver_hot_m[rows, :] = onehot_rows(column(receivers), mesh_rows)
        sum_hot_m[:, rows] = onehot_columns(receivers, mesh_rows)

    @pl.loop(0, count)
    def _(step):
        slots = held.mesh_slots[pl.ds(step, 1), :]
        pick_hot_m[rows_at(step * cap_m, cap_m), :] = onehot_rows(column(slots), mesh_rows)

    @pl.loop(0, mesh_edge_rows // BLOCK)
    def _(step):
        rows = rows_at(step * BLOCK, BLOCK)
        preact_m[rows, :] = dot(
            held.mesh_edges[rows, :], held.process_edge_in[:width, :]
        )

    ready(copies.encode_node_in)
    node_preact = dot(held.mesh_latent[...], held.encode_node_in[:width, :])
    ready(copies.encode_edge_vectors, copies.encode_edge_out, copies.encode_node_vectors, copies.encode_node_out)

    def wait_for(first, size):
        @pl.loop(0, size)
        def _(index):
            @pl.when(first + index != me)
            def _():
                grid_copy(lax.rem(me + 1, count), first + index).wait_recv()

    def gathered(rows, first, size):
        span = rows_at(first * cap_g, size * cap_g, 128)
        return dot(sender_hot[rows, span], arrived[span, :])

    half = count // 2
    quarter = half // 2
    other = (1 - my_half) * half
    stages = (
        (my_half * half, half),
        (other + my_quarter * quarter, quarter),
        (other + (1 - my_quarter) * quarter, quarter),
    )
    for first, size in stages[:2]:
        wait_for(first, size)

        @pl.loop(0, grid_edge_rows // BLOCK, unroll=3)
        def _(step, first=first, size=size):
            rows = rows_at(step * BLOCK, BLOCK)
            preact[rows, :] += gathered(rows, first, size)

    wait_for(*stages[2])

    @pl.loop(0, grid_edge_rows // BLOCK, unroll=3)
    def _(step):
        rows = rows_at(step * BLOCK, BLOCK)
        total = preact[rows, :] + gathered(rows, *stages[2])
        update = branch(total, held.encode_edge_vectors, held.encode_edge_out)
        message[rows, :] = (held.grid_edges[rows, :].astype(F32) + update).astype(BF)

    encode_sum = dot(sum_hot[...], message[...]).astype(BF)
    node_preact = node_preact + dot(encode_sum, held.encode_node_in[width:, :])
    middle = (
        held.mesh_latent[...].astype(F32)
        + branch(node_preact, held.encode_node_vectors, held.encode_node_out)
    ).astype(BF)

    own_mesh = dot(middle, held.process_edge_in[width : 2 * width, :]).astype(BF)
    table[rim_held : rim_held + mesh_rows, :] = own_mesh

    def far_copy(target, source):
        return pltpu.make_async_remote_copy(
            src_ref=send_m.at[rows_at(target * cap_m, cap_m)],
            dst_ref=table.at[rows_at(near + source * cap_m, cap_m)],
            send_sem=send_sem_m.at[target],
            recv_sem=recv_sem_m.at[source],
            device_id={"band": target},
            device_id_type=MESH,
        )

    size_m = group_size(count, cap_m)
    groups_m = count // size_m

    @pl.loop(0, groups_m)
    def _(step):
        group = lax.rem(me // size_m + groups_m // 2 + step, groups_m)
        rows = rows_at(group * size_m * cap_m, size_m * cap_m)
        send_m[rows, :] = dot(pick_hot_m[rows, :], own_mesh).astype(BF)

        @pl.loop(0, size_m)
        def _(j):
            target = group * size_m + j

            @pl.when(target != me)
            def _():
                far_copy(target, me).start()

    to_right = pltpu.make_async_remote_copy(
        src_ref=table.at[pl.ds(rim_held + mesh_rows - rim_held, rim_held)],
        dst_ref=table.at[pl.ds(0, rim_held)],
        send_sem=send_sem_rim.at[0],
        recv_sem=recv_sem_rim.at[0],
        device_id={"band": lax.rem(me + 1, count)},
        device_id_type=MESH,
    )
    to_left = pltpu.make_async_remote_copy(
        src_ref=table.at[pl.ds(rim_held, rim_held)],
        dst_ref=table.at[pl.ds(rim_held + mesh_rows, rim_held)],
        send_sem=send_sem_rim.at[1],
        recv_sem=recv_sem_rim.at[1],
        device_id={"band": lax.rem(me + count - 1, count)},
        device_id_type=MESH,
    )
    to_right.start()
    to_left.start()
    table[rows_at(near + me * cap_m, cap_m), :] = send_m[rows_at(me * cap_m, cap_m), :]

    middle_terms = dot(middle, held.process_edge_in[2 * width :, :]).astype(BF)

    @pl.loop(0, mesh_edge_rows // BLOCK)
    def _(step):
        rows = rows_at(step * BLOCK, BLOCK)
        preact_m[rows, :] += dot(receiver_hot_m[rows, :], middle_terms)

    ready(copies.process_edge_vectors, copies.process_edge_out)
    ready(copies.process_node_in, copies.process_node_vectors, copies.process_node_out)
    node_preact = dot(middle, held.process_node_in[:width, :])

    to_right.wait_recv()
    to_left.wait_recv()

    def wait_far(first):
        @pl.loop(first, first + half)
        def _(source):
            @pl.when(source != me)
            def _():
                far_copy(lax.rem(me + 1, count), source).wait_recv()

    def far(rows, first):
        span = rows_at(near + first * cap_m, half * cap_m, 128)
        return dot(sender_hot_m[rows, span], table[span, :])

    wait_far(my_half * half)

    @pl.loop(0, mesh_edge_rows // BLOCK, unroll=4)
    def _(step):
        rows = rows_at(step * BLOCK, BLOCK)
        preact_m[rows, :] += dot(sender_hot_m[rows, :near], table[:near, :]) + far(
            rows, my_half * half
        )

    wait_far(other)

    @pl.loop(0, mesh_edge_rows // BLOCK, unroll=4)
    def _(step):
        rows = rows_at(step * BLOCK, BLOCK)
        total = preact_m[rows, :] + far(rows, other)
        update = branch(total, held.process_edge_vectors, held.process_edge_out)
        message[rows, :] = (held.mesh_edges[rows, :].astype(F32) + update).astype(BF)

    process_sum = dot(sum_hot_m[...], message[:mesh_edge_rows, :]).astype(BF)
    node_preact = node_preact + dot(process_sum, held.process_node_in[width:, :])
    mesh_result[...] = (
        middle.astype(F32)
        + branch(node_preact, held.process_node_vectors, held.process_node_out)
    ).astype(BF)
    mesh_store = pltpu.make_async_copy(mesh_result, mesh_out, out_sem.at[1])
    mesh_store.start()

    @pl.loop(0, count)
    def _(target):
        @pl.when(target != me)
        def _():
            grid_copy(target, 0).wait_send()
            far_copy(target, 0).wait_send()

    to_right.wait_send()
    to_left.wait_send()
    grid_store.wait()
    mesh_store.wait()


def pad_slots(slots, cap):
    slots = slots[0]
    if cap == slots.shape[1]:
        return slots
    return jnp.pad(slots, ((0, 0), (0, cap - slots.shape[1])), constant_values=-1)


def spread_codes(codes, slots, cap):
    return codes if cap == slots else codes // slots * cap + codes % slots


def local(*operands):
    args = Operands(*operands)
    count = lax.axis_size("band")
    slots_g = args.grid_slots.shape[2]
    slots_m = args.mesh_slots.shape[2]
    cap_g, cap_m = round_up(slots_g, 16), round_up(slots_m, 16)
    mesh_rows, width = args.mesh_latent.shape
    mesh_senders = args.mesh_senders
    if cap_m != slots_m:
        first = mesh_rows + 2 * (mesh_rows // 4)
        far = first + spread_codes(mesh_senders - first, slots_m, cap_m)
        mesh_senders = jnp.where(mesh_senders < first, mesh_senders, far)
    args = args._replace(
        grid_slots=pad_slots(args.grid_slots, cap_g),
        mesh_slots=pad_slots(args.mesh_slots, cap_m),
        grid_senders=spread_codes(args.grid_senders, slots_g, cap_g).reshape(-1, 128),
        grid_receivers=args.grid_receivers.reshape(-1, 128),
        mesh_senders=mesh_senders.reshape(-1, 128),
        mesh_receivers=args.mesh_receivers.reshape(-1, 128),
    )
    grid_rows = args.grid_latent.shape[0]
    grid_edge_rows = args.grid_edges.shape[0]
    mesh_edge_rows = args.mesh_edges.shape[0]
    near = mesh_rows + 2 * round_up(mesh_rows // 4, 16)
    edge_rows = max(grid_edge_rows, mesh_edge_rows)
    dma = pltpu.SemaphoreType.DMA
    anywhere = pl.BlockSpec(memory_space=pl.ANY)
    scratch = [pltpu.VMEM(arg.shape, arg.dtype) for arg in args]
    scratch += [
        pltpu.VMEM((grid_rows, width), BF),
        pltpu.VMEM((count * cap_g, width), BF),
        pltpu.VMEM((count * cap_g, width), BF),
        pltpu.VMEM((grid_edge_rows, count * cap_g), BF),
        pltpu.VMEM((grid_edge_rows, mesh_rows), BF),
        pltpu.VMEM((mesh_rows, grid_edge_rows), BF),
        pltpu.VMEM((grid_edge_rows, width), F32),
        pltpu.VMEM((edge_rows, width), BF),
        pltpu.VMEM((grid_rows, width), BF),
        pltpu.VMEM((count * cap_m, width), BF),
        pltpu.VMEM((near + count * cap_m, width), BF),
        pltpu.VMEM((mesh_edge_rows, near + count * cap_m), BF),
        pltpu.VMEM((mesh_edge_rows, mesh_rows), BF),
        pltpu.VMEM((mesh_rows, mesh_edge_rows), BF),
        pltpu.VMEM((count * cap_m, mesh_rows), BF),
        pltpu.VMEM((mesh_edge_rows, width), F32),
        pltpu.VMEM((mesh_rows, width), BF),
        dma((COUNT,)),
        dma((2,)),
        dma((count,)),
        dma((count,)),
        dma((count,)),
        dma((count,)),
        dma((2,)),
        dma((2,)),
    ]
    return pl.pallas_call(
        functools.partial(kernel, (count, cap_g, cap_m)),
        out_shape=(
            jax.ShapeDtypeStruct((grid_rows, width), BF),
            jax.ShapeDtypeStruct((mesh_rows, width), BF),
        ),
        in_specs=[anywhere] * COUNT,
        out_specs=(anywhere, anywhere),
        scratch_shapes=scratch,
        compiler_params=pltpu.CompilerParams(
            collective_id=0, has_side_effects=True, vmem_limit_bytes=56 * 1024 * 1024
        ),
    )(*args)


def solution(mesh):
    return jax.shard_map(
        local,
        mesh=mesh,
        in_specs=(
            P(("groups", "band"), None),
            P(("groups", "band"), None),
            P("band", None),
            P("band", None),
            P("band", None, None),
            P("band"),
            P("band"),
            P("band", None, None),
            P("band"),
            P("band"),
            P(),
            P(),
            P(),
            P(),
            P(),
            P(),
            P(),
            P(),
            P(),
            P(),
            P(),
            P(),
            P(),
            P(),
            P(),
        ),
        out_specs=(P(("groups", "band"), None), P(("groups", "band"), None)),
        check_vma=False,
    )
```

```python
import functools
import typing
from typing import Any

import jax
import jax.numpy as jnp
from jax import lax
from jax.experimental import pallas as pl
from jax.experimental.pallas import tpu as pltpu
from jax.sharding import PartitionSpec as P

MESH = pl.DeviceIdType.MESH
BF = jnp.bfloat16
F32 = jnp.float32
BLOCK = 256

class Operands(typing.NamedTuple):
    grid_latent: Any
    mesh_latent: Any
    grid_edges: Any
    mesh_edges: Any
    grid_slots: Any
    grid_senders: Any
    grid_receivers: Any
    mesh_slots: Any
    mesh_senders: Any
    mesh_receivers: Any
    grid_node_in: Any
    grid_node_out: Any
    grid_node_vectors: Any
    encode_edge_in: Any
    encode_edge_out: Any
    encode_edge_vectors: Any
    encode_node_in: Any
    encode_node_out: Any
    encode_node_vectors: Any
    process_edge_in: Any
    process_edge_out: Any
    process_edge_vectors: Any
    process_node_in: Any
    process_node_out: Any
    process_node_vectors: Any


COUNT = len(Operands._fields)


def round_up(value, unit):
    return (value + unit - 1) // unit * unit


def group_size(count, rows):
    size = 1
    while size * 2 <= count and size * 2 * rows <= BLOCK:
        size *= 2
    return size


def dot(left, right):
    return jnp.dot(left, right, preferred_element_type=F32)


def branch(preact, vectors, weight_out):
    half = 0.5 * (preact + vectors[0:1, :])
    hidden = (half + half * jnp.tanh(half)).astype(BF)
    output = dot(hidden, weight_out[...])
    centred = output - jnp.mean(output, axis=-1, keepdims=True)
    spread = jnp.mean(centred * centred, axis=-1, keepdims=True)
    return centred * lax.rsqrt(spread + 1e-05) * vectors[1:2, :]


def column(row):
    n = row.shape[1]
    eye = lax.broadcasted_iota(jnp.int32, (n, n), 0) == lax.broadcasted_iota(
        jnp.int32, (n, n), 1
    )
    spread = jnp.where(eye, jnp.broadcast_to(row.astype(F32), (n, n)), 0.0)
    return jnp.sum(spread, axis=1, keepdims=True)


def onehot_rows(col, width):
    ids = lax.broadcasted_iota(jnp.int32, (1, width), 1).astype(F32)
    return jnp.where(col == ids, 1.0, 0.0).astype(BF)


def onehot_columns(row, height):
    ids = lax.broadcasted_iota(jnp.int32, (height, 1), 0).astype(F32)
    return jnp.where(ids == row.astype(F32), 1.0, 0.0).astype(BF)


def rows_at(start, size, unit=16):
    return pl.ds(pl.multiple_of(start, unit), size)


def kernel(dims, *refs):
    count, cap_g, cap_m = dims
    n_in = COUNT
    hbm = Operands(*refs[:n_in])
    grid_out, mesh_out = refs[n_in : n_in + 2]
    held = Operands(*refs[n_in + 2 : 2 * n_in + 2])
    (
        own_terms,
        send_g,
        arrived,
        sender_hot,
        receiver_hot,
        sum_hot,
        preact,
        message,
        grid_result,
        send_m,
        table,
        sender_hot_m,
        receiver_hot_m,
        sum_hot_m,
        pick_hot_m,
        preact_m,
        mesh_result,
        fetch_sem,
        out_sem,
        send_sem,
        recv_sem,
        send_sem_m,
        recv_sem_m,
        send_sem_rim,
        recv_sem_rim,
    ) = refs[2 * n_in + 2 :]
    me = lax.axis_index("band")
    width = held.grid_latent.shape[1]
    grid_rows = held.grid_latent.shape[0]
    mesh_rows = held.mesh_latent.shape[0]
    grid_edge_rows = held.grid_edges.shape[0]
    mesh_edge_rows = held.mesh_edges.shape[0]
    rim = mesh_rows // 4
    rim_held = round_up(rim, 16)
    near = mesh_rows + 2 * rim_held

    copies = Operands(
        *[
            pltpu.make_async_copy(hbm[index], held[index], fetch_sem.at[index])
            for index in range(n_in)
        ]
    )
    for copy in (
        copies.grid_slots,
        copies.grid_latent,
        copies.encode_edge_in,
        copies.grid_senders,
        copies.grid_receivers,
        copies.mesh_latent,
        copies.grid_edges,
        copies.grid_node_in,
        copies.grid_node_vectors,
        copies.grid_node_out,
        copies.mesh_slots,
        copies.mesh_senders,
        copies.mesh_receivers,
        copies.mesh_edges,
        copies.process_edge_in,
        copies.encode_node_in,
        copies.encode_edge_vectors,
        copies.encode_edge_out,
        copies.encode_node_vectors,
        copies.encode_node_out,
        copies.process_edge_vectors,
        copies.process_edge_out,
        copies.process_node_in,
        copies.process_node_vectors,
        copies.process_node_out,
    ):
        copy.start()

    barrier = pltpu.get_barrier_semaphore()

    @pl.loop(1, count)
    def _(step):
        pl.semaphore_signal(
            barrier,
            inc=1,
            device_id={"band": lax.rem(me + step, count)},
            device_id_type=MESH,
        )

    def ready(*wanted):
        for copy in wanted:
            copy.wait()

    ready(copies.grid_slots, copies.grid_latent, copies.encode_edge_in)

    @pl.loop(0, grid_rows // BLOCK)
    def _(step):
        rows = rows_at(step * BLOCK, BLOCK)
        own_terms[rows, :] = dot(
            held.grid_latent[rows, :], held.encode_edge_in[width : 2 * width, :]
        ).astype(BF)

    pl.semaphore_wait(barrier, count - 1)

    size_g = group_size(count, cap_g)
    groups_g = count // size_g
    my_group = me // size_g
    half_groups = groups_g // 2
    quarter_groups = half_groups // 2
    my_half, my_local = my_group // half_groups, lax.rem(my_group, half_groups)
    my_quarter = my_local // quarter_groups

    def grid_copy(target, source):
        return pltpu.make_async_remote_copy(
            src_ref=send_g.at[rows_at(target * cap_g, cap_g)],
            dst_ref=arrived.at[rows_at(source * cap_g, cap_g)],
            send_sem=send_sem.at[target],
            recv_sem=recv_sem.at[source],
            device_id={"band": target},
            device_id_type=MESH,
        )

    @pl.loop(0, groups_g)
    def _(step):
        half = lax.rem(my_half + 1 + step // half_groups, 2)
        turn = lax.rem(step, half_groups)
        quarter = lax.rem(my_quarter + turn // quarter_groups, 2)
        group = (
            half * half_groups
            + quarter * quarter_groups
            + lax.rem(my_local + turn, quarter_groups)
        )
        hot = [
            onehot_rows(
                column(held.grid_slots[pl.ds(group * size_g + j, 1), :]), grid_rows
            )
            for j in range(size_g)
        ]
        hot = jnp.concatenate(hot, axis=0) if size_g > 1 else hot[0]
        picked = dot(hot, own_terms[...]).astype(BF)
        send_g[rows_at(group * size_g * cap_g, size_g * cap_g), :] = picked
        @pl.loop(0, size_g)
        def _(j):
            target = group * size_g + j

            @pl.when(target != me)
            def _():
                grid_copy(target, me).start()

    arrived[rows_at(me * cap_g, cap_g), :] = send_g[rows_at(me * cap_g, cap_g), :]

    ready(copies.grid_senders, copies.grid_receivers, copies.mesh_latent, copies.grid_edges)
    receiver_terms = dot(
        held.mesh_latent[...], held.encode_edge_in[2 * width :, :]
    ).astype(BF)

    @pl.loop(0, grid_edge_rows // 128)
    def _(step):
        rows = rows_at(step * 128, 128, 128)
        codes = held.grid_senders[pl.ds(step, 1), :]
        sender_hot[rows, :] = onehot_rows(column(codes), count * cap_g)
        receivers = held.grid_receivers[pl.ds(step, 1), :]
        receiver_hot[rows, :] = onehot_rows(column(receivers), mesh_rows)
        sum_hot[:, rows] = onehot_columns(receivers, mesh_rows)

    @pl.loop(0, grid_edge_rows // BLOCK)
    def _(step):
        rows = rows_at(step * BLOCK, BLOCK)
        preact[rows, :] = dot(
            held.grid_edges[rows, :], held.encode_edge_in[:width, :]
        ) + dot(receiver_hot[rows, :], receiver_terms)

    ready(copies.grid_node_in, copies.grid_node_vectors, copies.grid_node_out)

    @pl.loop(0, grid_rows // BLOCK)
    def _(step):
        rows = rows_at(step * BLOCK, BLOCK)
        latent = held.grid_latent[rows, :]
        update = branch(
            dot(latent, held.grid_node_in[...]),
            held.grid_node_vectors,
            held.grid_node_out,
        )
        grid_result[rows, :] = (latent.astype(F32) + update).astype(BF)

    grid_store = pltpu.make_async_copy(grid_result, grid_out, out_sem.at[0])
    grid_store.start()

    ready(copies.mesh_slots, copies.mesh_senders, copies.mesh_receivers, copies.mesh_edges, copies.process_edge_in)
    near_codes = mesh_rows + 2 * rim

    @pl.loop(0, mesh_edge_rows // 128)
    def _(step):
        rows = rows_at(step * 128, 128, 128)
        codes = held.mesh_senders[pl.ds(step, 1), :]
        shift = rim_held - rim
        codes = codes + jnp.where(codes < near_codes, shift, 2 * shift)
        sender_hot_m[rows, :] = onehot_rows(column(codes), near + count * cap_m)
        receivers = held.mesh_receivers[pl.ds(step, 1), :]
        receiver_hot_m[rows, :] = onehot_rows(column(receivers), mesh_rows)
        sum_hot_m[:, rows] = onehot_columns(receivers, mesh_rows)

    @pl.loop(0, count)
    def _(step):
        slots = held.mesh_slots[pl.ds(step, 1), :]
        pick_hot_m[rows_at(step * cap_m, cap_m), :] = onehot_rows(column(slots), mesh_rows)

    @pl.loop(0, mesh_edge_rows // BLOCK)
    def _(step):
        rows = rows_at(step * BLOCK, BLOCK)
        preact_m[rows, :] = dot(
            held.mesh_edges[rows, :], held.process_edge_in[:width, :]
        )

    ready(copies.encode_node_in)
    node_preact = dot(held.mesh_latent[...], held.encode_node_in[:width, :])
    ready(copies.encode_edge_vectors, copies.encode_edge_out, copies.encode_node_vectors, copies.encode_node_out)

    def wait_for(first, size):
        @pl.loop(0, size)
        def _(index):
            @pl.when(first + index != me)
            def _():
                grid_copy(lax.rem(me + 1, count), first + index).wait_recv()

    def gathered(rows, first, size):
        span = rows_at(first * cap_g, size * cap_g, 128)
        return dot(sender_hot[rows, span], arrived[span, :])

    half = count // 2
    quarter = half // 2
    other = (1 - my_half) * half
    stages = (
        (my_half * half, half),
        (other + my_quarter * quarter, quarter),
        (other + (1 - my_quarter) * quarter, quarter),
    )
    for first, size in stages[:2]:
        wait_for(first, size)

        @pl.loop(0, grid_edge_rows // BLOCK, unroll=3)
        def _(step, first=first, size=size):
            rows = rows_at(step * BLOCK, BLOCK)
            preact[rows, :] += gathered(rows, first, size)

    wait_for(*stages[2])

    @pl.loop(0, grid_edge_rows // BLOCK, unroll=6)
    def _(step):
        rows = rows_at(step * BLOCK, BLOCK)
        total = preact[rows, :] + gathered(rows, *stages[2])
        update = branch(total, held.encode_edge_vectors, held.encode_edge_out)
        message[rows, :] = (held.grid_edges[rows, :].astype(F32) + update).astype(BF)

    encode_sum = dot(sum_hot[...], message[...]).astype(BF)
    node_preact = node_preact + dot(encode_sum, held.encode_node_in[width:, :])
    middle = (
        held.mesh_latent[...].astype(F32)
        + branch(node_preact, held.encode_node_vectors, held.encode_node_out)
    ).astype(BF)

    own_mesh = dot(middle, held.process_edge_in[width : 2 * width, :]).astype(BF)
    table[rim_held : rim_held + mesh_rows, :] = own_mesh

    def far_copy(target, source):
        return pltpu.make_async_remote_copy(
            src_ref=send_m.at[rows_at(target * cap_m, cap_m)],
            dst_ref=table.at[rows_at(near + source * cap_m, cap_m)],
            send_sem=send_sem_m.at[target],
            recv_sem=recv_sem_m.at[source],
            device_id={"band": target},
            device_id_type=MESH,
        )

    size_m = group_size(count, cap_m)
    groups_m = count // size_m

    @pl.loop(0, groups_m)
    def _(step):
        group = lax.rem(me // size_m + groups_m // 2 + step, groups_m)
        rows = rows_at(group * size_m * cap_m, size_m * cap_m)
        send_m[rows, :] = dot(pick_hot_m[rows, :], own_mesh).astype(BF)

        @pl.loop(0, size_m)
        def _(j):
            target = group * size_m + j

            @pl.when(target != me)
            def _():
                far_copy(target, me).start()

    to_right = pltpu.make_async_remote_copy(
        src_ref=table.at[pl.ds(rim_held + mesh_rows - rim_held, rim_held)],
        dst_ref=table.at[pl.ds(0, rim_held)],
        send_sem=send_sem_rim.at[0],
        recv_sem=recv_sem_rim.at[0],
        device_id={"band": lax.rem(me + 1, count)},
        device_id_type=MESH,
    )
    to_left = pltpu.make_async_remote_copy(
        src_ref=table.at[pl.ds(rim_held, rim_held)],
        dst_ref=table.at[pl.ds(rim_held + mesh_rows, rim_held)],
        send_sem=send_sem_rim.at[1],
        recv_sem=recv_sem_rim.at[1],
        device_id={"band": lax.rem(me + count - 1, count)},
        device_id_type=MESH,
    )
    to_right.start()
    to_left.start()
    table[rows_at(near + me * cap_m, cap_m), :] = send_m[rows_at(me * cap_m, cap_m), :]

    middle_terms = dot(middle, held.process_edge_in[2 * width :, :]).astype(BF)

    @pl.loop(0, mesh_edge_rows // BLOCK)
    def _(step):
        rows = rows_at(step * BLOCK, BLOCK)
        preact_m[rows, :] += dot(receiver_hot_m[rows, :], middle_terms)

    ready(copies.process_edge_vectors, copies.process_edge_out)
    ready(copies.process_node_in, copies.process_node_vectors, copies.process_node_out)
    node_preact = dot(middle, held.process_node_in[:width, :])

    to_right.wait_recv()
    to_left.wait_recv()

    def wait_far(first):
        @pl.loop(first, first + half)
        def _(source):
            @pl.when(source != me)
            def _():
                far_copy(lax.rem(me + 1, count), source).wait_recv()

    def far(rows, first):
        span = rows_at(near + first * cap_m, half * cap_m, 128)
        return dot(sender_hot_m[rows, span], table[span, :])

    wait_far(my_half * half)

    @pl.loop(0, mesh_edge_rows // BLOCK, unroll=4)
    def _(step):
        rows = rows_at(step * BLOCK, BLOCK)
        preact_m[rows, :] += dot(sender_hot_m[rows, :near], table[:near, :]) + far(
            rows, my_half * half
        )

    wait_far(other)

    @pl.loop(0, mesh_edge_rows // BLOCK, unroll=4)
    def _(step):
        rows = rows_at(step * BLOCK, BLOCK)
        total = preact_m[rows, :] + far(rows, other)
        update = branch(total, held.process_edge_vectors, held.process_edge_out)
        message[rows, :] = (held.mesh_edges[rows, :].astype(F32) + update).astype(BF)

    process_sum = dot(sum_hot_m[...], message[:mesh_edge_rows, :]).astype(BF)
    node_preact = node_preact + dot(process_sum, held.process_node_in[width:, :])
    mesh_result[...] = (
        middle.astype(F32)
        + branch(node_preact, held.process_node_vectors, held.process_node_out)
    ).astype(BF)
    mesh_store = pltpu.make_async_copy(mesh_result, mesh_out, out_sem.at[1])
    mesh_store.start()

    @pl.loop(0, count)
    def _(target):
        @pl.when(target != me)
        def _():
            grid_copy(target, 0).wait_send()
            far_copy(target, 0).wait_send()

    to_right.wait_send()
    to_left.wait_send()
    grid_store.wait()
    mesh_store.wait()


def pad_slots(slots, cap):
    slots = slots[0]
    if cap == slots.shape[1]:
        return slots
    return jnp.pad(slots, ((0, 0), (0, cap - slots.shape[1])), constant_values=-1)


def spread_codes(codes, slots, cap):
    return codes if cap == slots else codes // slots * cap + codes % slots


def local(*operands):
    args = Operands(*operands)
    count = lax.axis_size("band")
    slots_g = args.grid_slots.shape[2]
    slots_m = args.mesh_slots.shape[2]
    cap_g, cap_m = round_up(slots_g, 16), round_up(slots_m, 16)
    mesh_rows, width = args.mesh_latent.shape
    mesh_senders = args.mesh_senders
    if cap_m != slots_m:
        first = mesh_rows + 2 * (mesh_rows // 4)
        far = first + spread_codes(mesh_senders - first, slots_m, cap_m)
        mesh_senders = jnp.where(mesh_senders < first, mesh_senders, far)
    args = args._replace(
        grid_slots=pad_slots(args.grid_slots, cap_g),
        mesh_slots=pad_slots(args.mesh_slots, cap_m),
        grid_senders=spread_codes(args.grid_senders, slots_g, cap_g).reshape(-1, 128),
        grid_receivers=args.grid_receivers.reshape(-1, 128),
        mesh_senders=mesh_senders.reshape(-1, 128),
        mesh_receivers=args.mesh_receivers.reshape(-1, 128),
    )
    grid_rows = args.grid_latent.shape[0]
    grid_edge_rows = args.grid_edges.shape[0]
    mesh_edge_rows = args.mesh_edges.shape[0]
    near = mesh_rows + 2 * round_up(mesh_rows // 4, 16)
    edge_rows = max(grid_edge_rows, mesh_edge_rows)
    dma = pltpu.SemaphoreType.DMA
    anywhere = pl.BlockSpec(memory_space=pl.ANY)
    scratch = [pltpu.VMEM(arg.shape, arg.dtype) for arg in args]
    scratch += [
        pltpu.VMEM((grid_rows, width), BF),
        pltpu.VMEM((count * cap_g, width), BF),
        pltpu.VMEM((count * cap_g, width), BF),
        pltpu.VMEM((grid_edge_rows, count * cap_g), BF),
        pltpu.VMEM((grid_edge_rows, mesh_rows), BF),
        pltpu.VMEM((mesh_rows, grid_edge_rows), BF),
        pltpu.VMEM((grid_edge_rows, width), F32),
        pltpu.VMEM((edge_rows, width), BF),
        pltpu.VMEM((grid_rows, width), BF),
        pltpu.VMEM((count * cap_m, width), BF),
        pltpu.VMEM((near + count * cap_m, width), BF),
        pltpu.VMEM((mesh_edge_rows, near + count * cap_m), BF),
        pltpu.VMEM((mesh_edge_rows, mesh_rows), BF),
        pltpu.VMEM((mesh_rows, mesh_edge_rows), BF),
        pltpu.VMEM((count * cap_m, mesh_rows), BF),
        pltpu.VMEM((mesh_edge_rows, width), F32),
        pltpu.VMEM((mesh_rows, width), BF),
        dma((COUNT,)),
        dma((2,)),
        dma((count,)),
        dma((count,)),
        dma((count,)),
        dma((count,)),
        dma((2,)),
        dma((2,)),
    ]
    return pl.pallas_call(
        functools.partial(kernel, (count, cap_g, cap_m)),
        out_shape=(
            jax.ShapeDtypeStruct((grid_rows, width), BF),
            jax.ShapeDtypeStruct((mesh_rows, width), BF),
        ),
        in_specs=[anywhere] * COUNT,
        out_specs=(anywhere, anywhere),
        scratch_shapes=scratch,
        compiler_params=pltpu.CompilerParams(
            collective_id=0, has_side_effects=True, vmem_limit_bytes=56 * 1024 * 1024
        ),
    )(*args)


def solution(mesh):
    return jax.shard_map(
        local,
        mesh=mesh,
        in_specs=(
            P(("groups", "band"), None),
            P(("groups", "band"), None),
            P("band", None),
            P("band", None),
            P("band", None, None),
            P("band"),
            P("band"),
            P("band", None, None),
            P("band"),
            P("band"),
            P(),
            P(),
            P(),
            P(),
            P(),
            P(),
            P(),
            P(),
            P(),
            P(),
            P(),
            P(),
            P(),
            P(),
            P(),
        ),
        out_specs=(P(("groups", "band"), None), P(("groups", "band"), None)),
        check_vma=False,
    )
```
